512 devices in a mesh: mp: 64 (over y, z_hi, core), server: 8 (over x, z_lo).
Axes of the slice: x: 4, y: 8, z: 8 (z_hi: 4, z_lo: 2; z = z_hi * 2 + z_lo), core: 2. Of those that a mesh axis runs over, the one named last changes fastest.
Arguments:
- velocity_start: float32 [2, 4096, 1024], P(None, 'mp', 'server'), may hold values from -6 to 6
- stress_start: float32 [3, 4096, 1024], P(None, 'mp', 'server'), may hold values from -6 to 6
- wind_stress: float32 [2, 4096, 1024], P(None, 'mp', 'server'), may hold values from -6 to 6
- strength: float32 [4096, 1024], P('mp', 'server'), may hold values from 0.5 to 2
- ice_mass: float32 [4096, 1024], P('mp', 'server'), may hold values from 0.5 to 2
- ice_mask: int32 [4096, 1024], P('mp', 'server'), may hold values from 0 to 1, as said below
- send_list: int32 [64, 8, 5, 8], P('mp', 'server'), may hold values from 0 to 63
- block_index: int32 [64, 8, 8, 4], P('mp', 'server'), may hold values from 0 to 39, as said below
- span_slot: int32 [64, 8, 8], P('mp', 'server'), may hold values from 0 to 7, each once within a row
- remap_weights: bfloat16 [64, 8, 8, 4, 128, 128], P('mp', 'server'), may hold values from 0 to 0.00390625
Outputs:
- model_state: float32 [5, 4096, 1024], P(None, 'mp', 'server')
- written: float32 [64, 8, 6, 8, 128], P('mp', 'server')
The draws below stay inside these ranges and needn't reach their ends.
Inputs may be any that keep to these rules, and one draw needn't show every extreme that they name: `ice_mask`: 1 marks an ice-covered cell. The device d + 2 - block_index // 8 along mp always exists.
All inputs are finite; a program needn't handle non-finite values.
Results may differ from the reference program's by a relative error of at most 0.00075.
Values may be sent and summed in bfloat16 or wider, within the bound.
A program may use at most 64 MiB of HBM per device.

```python
import math
import jax
import jax.numpy as jnp
from jax import lax

CY = 64
CX = 128
ITERS = 20
REACH = 2
CAP = 8
R = 8
K = 4
DB = 128
OFFSETS = 5
NY = 4096
NX = 1024
TILES_Y = 64
TILES_X = 8
N_MP = 64
N_SERVER = 8


def draw_ice_mask(key, part):
    key = jax.random.fold_in(key, 3)
    first_key, second_key = jax.random.split(key)
    level = jax.random.randint(first_key, (NY, 1), 0, 1001)
    cutoff = level * level // 1000
    sample = jax.random.randint(second_key, (NY, NX), 0, 1000)
    return (sample < cutoff).astype(jnp.int32)


def draw_block_index(key, part):
    key = jax.random.fold_in(key, 7)
    first_key, second_key = jax.random.split(key)
    shape = (N_MP, N_SERVER, R, K)
    distance = jax.random.randint(first_key, shape, -REACH, REACH + 1)
    device_row = jnp.arange(N_MP, dtype=jnp.int32).reshape(N_MP, 1, 1, 1)
    source = jnp.clip(device_row - distance, 0, N_MP - 1)
    offset = device_row - source + REACH
    slot_index = jax.random.randint(second_key, shape, 0, CAP)
    return (offset * CAP + slot_index).astype(jnp.int32)


def plant(values, rng, smallest, high):
    spot = [jax.random.randint(jax.random.fold_in(rng, axis), (), 0, length) for axis, length in enumerate(values.shape)]
    widest = values.shape.index(max(values.shape))
    next_to = spot[:widest] + [(spot[widest] + 1) % values.shape[widest]] + spot[widest + 1:]
    return values.at[tuple(spot)].set(smallest).at[tuple(next_to)].set(high)


def shard_levels(own_key, extent, cuts, smallest, largest):
    loudness = 1.0
    for axis_at, blocks in cuts:
        steps = jax.random.uniform(jax.random.fold_in(jax.random.fold_in(own_key, 6), axis_at), (blocks,), jnp.float32, smallest / len(cuts), largest / len(cuts))
        loudness = loudness * jnp.repeat(jnp.exp(steps), extent[axis_at] // blocks).reshape((-1,) + (1,) * (len(extent) - 1 - axis_at))
    return loudness


def normal_values(key, shape, spread, most, pieces=(), kind=jnp.bfloat16):
    values = spread * jax.random.normal(key, shape, jnp.float32)
    if pieces:
        values = values * shard_levels(key, shape, pieces, -0.22, 0.18)
    return jnp.clip(values, -most, most).astype(kind)


def setup_inputs(seed: int = 0) -> dict:
    splits = jax.random.split(jax.random.key(seed), 11)
    velocity_start = normal_values(splits[0], (2, NY, NX), 1.0, 6.0, ((1, 64), (2, 8)), jnp.float32)
    stress_start = normal_values(splits[1], (3, NY, NX), 1.0, 6.0, ((1, 64), (2, 8)), jnp.float32)
    wind_stress = normal_values(splits[2], (2, NY, NX), 1.0, 6.0, ((1, 64), (2, 8)), jnp.float32)
    strength = jnp.clip(jnp.exp(math.log(2.0) - 1.3862944 * jax.random.uniform(splits[3], (NY, NX), jnp.float32) ** shard_levels(splits[3], (NY, NX), ((0, 64), (1, 8)), -0.2, 0.2)), 0.5, 2.0)
    ice_mass = jnp.clip(jnp.exp(math.log(2.0) - 1.3862944 * jax.random.uniform(splits[4], (NY, NX), jnp.float32) ** shard_levels(splits[4], (NY, NX), ((0, 64), (1, 8)), -0.2, 0.2)), 0.5, 2.0)
    ice_mask = draw_ice_mask(jax.random.fold_in(splits[10], 71), 0)
    send_list = plant(jax.random.randint(splits[6], (TILES_Y, TILES_X, OFFSETS, CAP), 0, CY), jax.random.fold_in(splits[6], 1), 0, CY - 1).astype(jnp.int32)
    block_index = draw_block_index(jax.random.fold_in(splits[10], 71), 0)
    span_slot = jax.vmap(lambda own: jax.random.permutation(own, R))(jax.random.split(splits[8], TILES_Y * TILES_X)).reshape((TILES_Y, TILES_X, R)).astype(jnp.int32)
    remap_weights = jnp.clip(0.00390625 * jax.random.uniform(splits[9], (TILES_Y, TILES_X, R, K, CX, DB), jnp.float32) ** shard_levels(splits[9], (TILES_Y, TILES_X, R, K, CX, DB), ((0, 64), (1, 8)), -0.2, 0.2), 0.0, 0.00390625).astype(jnp.bfloat16)
    return {"velocity_start": velocity_start, "stress_start": stress_start, "wind_stress": wind_stress, "strength": strength, "ice_mass": ice_mass, "ice_mask": ice_mask, "send_list": send_list, "block_index": block_index, "span_slot": span_slot, "remap_weights": remap_weights}


RELAXATION = 0.1
STEP_SIZE = 0.3
DRAG_RATE = 1.0
DELTA_MIN = 0.5
ECC_SQUARED = 4.0
FRAC_FLOOR = 0.3

def trim_rim(array, amount):
    if amount == 0:
        return array
    return array[..., amount:array.shape[-2] - amount, amount:array.shape[-1] - amount]

def along_x(field):
    return (field[..., 1:-1, 2:] - field[..., 1:-1, :-2]) * 0.5

def along_y(field):
    return (field[..., 2:, 1:-1] - field[..., :-2, 1:-1]) * 0.5

def subcycle(fields, statics):
    statics_now = trim_rim(statics, (statics.shape[-1] - fields.shape[-1]) // 2)
    vel_x, vel_y, sig_one, sig_two, sig_shear = (fields[0], fields[1], fields[2], fields[3], fields[4])
    divergence = along_x(vel_x) + along_y(vel_y)
    tension = along_x(vel_x) - along_y(vel_y)
    shear_rate = along_y(vel_x) + along_x(vel_y)
    deform = jnp.sqrt(divergence * divergence + (tension * tension + shear_rate * shear_rate) / ECC_SQUARED)
    ice_load = trim_rim(statics_now[1] * statics_now[0], 1)
    bulk_visc = ice_load / (2.0 * (deform + DELTA_MIN))
    pressure = ice_load * deform / (deform + DELTA_MIN)
    new_one = (trim_rim(sig_one, 1) + RELAXATION * (bulk_visc * divergence - 0.5 * pressure)) / (1.0 + RELAXATION)
    new_two = (trim_rim(sig_two, 1) + RELAXATION * bulk_visc * tension / ECC_SQUARED) / (1.0 + RELAXATION)
    new_shear = (trim_rim(sig_shear, 1) + RELAXATION * bulk_visc * shear_rate / ECC_SQUARED) / (1.0 + RELAXATION)
    force_x = along_x(0.5 * (new_one + new_two)) + along_y(new_shear)
    force_y = along_x(new_shear) + along_y(0.5 * (new_one - new_two))
    interior = trim_rim(statics_now, 2)
    covered = interior[0] > 0.5
    next_x = jnp.where(covered, (trim_rim(vel_x, 2) + STEP_SIZE * (force_x + interior[3]) / interior[2]) / (1.0 + STEP_SIZE * DRAG_RATE), 0.0)
    next_y = jnp.where(covered, (trim_rim(vel_y, 2) + STEP_SIZE * (force_y + interior[4]) / interior[2]) / (1.0 + STEP_SIZE * DRAG_RATE), 0.0)
    stacked = jnp.stack([next_x, next_y, trim_rim(new_one, 1), trim_rim(new_two, 1), trim_rim(new_shear, 1)])
    return (stacked, trim_rim(pressure, 1))

def pad_grid(array, amount):
    return jnp.pad(array, ((0, 0), (amount, amount), (amount, amount)))

def reference(velocity_start, stress_start, wind_stress, strength, ice_mass, ice_mask, send_list, block_index, span_slot, remap_weights):
    ice_float = ice_mask.astype(jnp.float32)
    statics = pad_grid(jnp.stack([ice_float, strength, ice_mass, wind_stress[0], wind_stress[1]]), 2)
    fields = jnp.concatenate([velocity_start, stress_start], axis=0)
    pressure = jnp.zeros((NY, NX), jnp.float32)
    for step_index in range(ITERS):
        fields, pressure = subcycle(pad_grid(fields, 2), statics)
    field_rows = jnp.concatenate([fields, pressure[None], ice_float[None]], axis=0).astype(jnp.bfloat16)
    device_row = jnp.arange(N_MP, dtype=jnp.int32).reshape(N_MP, 1, 1, 1)
    column = jnp.arange(N_SERVER, dtype=jnp.int32).reshape(1, N_SERVER, 1, 1)
    offset = block_index // CAP
    slot_index = block_index % CAP
    source = device_row + REACH - offset
    grid_row = send_list[source, column, offset, slot_index]
    tile_view = field_rows.reshape(7, N_MP * CY, N_SERVER, CX)
    gathered = tile_view[:, source * CY + grid_row, column, :]
    gathered = jnp.moveaxis(gathered, 1, 0)

    def remap_device(pair):
        blocks, block_weights = pair
        return jnp.einsum('fsrkc,srkcq->sfrq', blocks.astype(jnp.float32), block_weights.astype(jnp.float32))
    totals = lax.map(remap_device, (gathered, remap_weights))
    remapped = totals[:, :, :6] / jnp.maximum(totals[:, :, 6:7], FRAC_FLOOR)
    inverse = jnp.argsort(span_slot, axis=-1).astype(jnp.int32)
    ordered = jnp.take_along_axis(remapped, inverse[:, :, None, :, None], axis=3)
    span_len = R // N_SERVER
    written = ordered.reshape(N_MP, N_SERVER, 6, N_SERVER, span_len, DB).transpose(0, 3, 2, 1, 4, 5).reshape(N_MP, N_SERVER, 6, R, DB)
    return (fields, written)
```

```python
import functools

import jax
import jax.numpy as jnp
from jax import lax
from jax.experimental import pallas as pl
from jax.experimental.pallas import tpu as pltpu
from jax.sharding import PartitionSpec as P

MESH = pl.DeviceIdType.MESH

CY, CX = 64, 128
ITERS = 20
HALO = 2 * ITERS
ROWS = CY + 2 * HALO
PAD = 8
FIELDS = 9
CAP, OFFSETS, BLOCKS, CROSS = 8, 5, 8, 4

RELAXATION = 0.1
STEP_SIZE = 0.3
DRAG_RATE = 1.0
FRAC_FLOOR = 0.3
KEEP_S = 1.0 / (1.0 + RELAXATION)
KEEP_V = 1.0 / (1.0 + STEP_SIZE * DRAG_RATE)
LOAD_SCALE = RELAXATION * 0.5 * KEEP_S
FORCE_SCALE = STEP_SIZE * KEEP_V * 0.25
WIND_SCALE = STEP_SIZE * KEEP_V
TINY = 1e-30

SIDE_ROWS = 3 * CY
CORNER_ROWS = 128
EDGE_ROWS = 368

SPATIAL = ((0, -1), (0, 1), (-1, 0), (1, 0), (-1, -1), (-1, 1), (1, -1), (1, 1))
AROUND = SPATIAL + ((-2, 0), (2, 0)) + tuple((0, k) for k in range(2, 7))


def rolled(x, amount):
    amount = amount % CX
    return x if amount == 0 else pltpu.roll(x, amount, 1)


def kernel(
    n_mp,
    n_server,
    vel_hbm,
    stress_hbm,
    wind_hbm,
    strength_hbm,
    mass_hbm,
    mask_hbm,
    send_list_hbm,
    block_index_hbm,
    span_slot_hbm,
    weights_hbm,
    state_hbm,
    written_ref,
    vel,
    stress,
    wind,
    strength,
    mass,
    mask,
    send_list,
    block_index,
    span_slot,
    weights,
    state,
    cells,
    moist,
    chosen,
    pressure,
    side_out,
    edge_out,
    corner_out,
    side_in,
    edge_in,
    corner_in,
    field_rows,
    rows_out,
    rows_in,
    rows_all,
    blocks_done,
    spans_out,
    spans_in,
    in_sem,
    weight_sem,
    state_sem,
    halo_send,
    halo_recv,
    rows_send,
    rows_recv,
    spans_send,
    spans_recv,
):
    me_y, me_x = lax.axis_index("mp"), lax.axis_index("server")

    def device(dy, dx):
        return (lax.rem(me_y + dy + n_mp, n_mp), lax.rem(me_x + dx + n_server, n_server))

    barrier = pltpu.get_barrier_semaphore()
    for dy, dx in AROUND:
        pl.semaphore_signal(barrier, inc=1, device_id=device(dy, dx), device_id_type=MESH)

    loads = [
        pltpu.make_async_copy(source, target, in_sem.at[i])
        for i, (source, target) in enumerate(
            (
                (vel_hbm, vel),
                (stress_hbm, stress),
                (wind_hbm, wind),
                (strength_hbm, strength),
                (mass_hbm, mass),
                (mask_hbm, mask),
                (send_list_hbm, send_list),
                (block_index_hbm, block_index),
                (span_slot_hbm, span_slot),
            )
        )
    ]
    for load in loads:
        load.start()
    weight_load = pltpu.make_async_copy(weights_hbm, weights, weight_sem)
    weight_load.start()
    for load in loads[:6]:
        load.wait()

    ice = mask[...].astype(jnp.float32)
    per_mass = ice / mass[...]
    own = [
        vel[0],
        vel[1],
        stress[0] + stress[1],
        stress[0] - stress[1],
        stress[2] * 2.0,
        strength[...] * ice * LOAD_SCALE,
        per_mass * FORCE_SCALE,
        wind[0] * per_mass * WIND_SCALE,
        wind[1] * per_mass * WIND_SCALE,
    ]
    lane = lax.broadcasted_iota(jnp.int32, (CY, CX), 1)
    spare = jnp.zeros((8, CX), jnp.float32)
    for f in range(FIELDS):
        cells[f, 0, PAD + HALO : PAD + HALO + CY] = own[f]
        for part in range(2):
            cells[f, part, 0:PAD] = spare
            cells[f, part, PAD + ROWS : PAD + ROWS + PAD] = spare
    edge_out[0] = jnp.concatenate([x[:HALO] for x in own] + [spare], axis=0).astype(jnp.bfloat16)
    edge_out[1] = jnp.concatenate([x[CY - HALO :] for x in own] + [spare], axis=0).astype(jnp.bfloat16)
    to_left, to_right = [], []
    for i in range(3):
        parts = [rolled(own[3 * k + i], 40 * k) for k in range(3)]
        to_left.append(jnp.where(lane < 40, parts[0], jnp.where(lane < 80, parts[1], parts[2])))
        to_right.append(jnp.where(lane >= 88, parts[0], jnp.where(lane < 40, parts[1], parts[2])))
    for side, packet in enumerate((to_left, to_right)):
        side_out[side] = jnp.concatenate(packet, axis=0).astype(jnp.bfloat16)
        corner_out[side] = jnp.concatenate([x[:HALO] for x in packet] + [spare], axis=0).astype(jnp.bfloat16)
        corner_out[2 + side] = jnp.concatenate([x[CY - HALO :] for x in packet] + [spare], axis=0).astype(jnp.bfloat16)

    pl.semaphore_wait(barrier, len(AROUND))

    sources = (
        side_out.at[0],
        side_out.at[1],
        edge_out.at[0],
        edge_out.at[1],
        corner_out.at[0],
        corner_out.at[1],
        corner_out.at[2],
        corner_out.at[3],
    )
    targets = (
        side_in.at[0],
        side_in.at[1],
        edge_in.at[0],
        edge_in.at[1],
        corner_in.at[0],
        corner_in.at[1],
        corner_in.at[2],
        corner_in.at[3],
    )
    halo = []
    for i, (dy, dx) in enumerate(SPATIAL):
        copy = pltpu.make_async_remote_copy(
            src_ref=sources[i],
            dst_ref=targets[i],
            send_sem=halo_send.at[i],
            recv_sem=halo_recv.at[i],
            device_id=device(dy, dx),
            device_id_type=MESH,
        )
        copy.start()
        halo.append(copy)
    for load in loads[6:]:
        load.wait()
    column = lax.broadcasted_iota(jnp.int32, (8, 8 * CY), 1) - CY * lax.broadcasted_iota(jnp.int32, (8, 8 * CY), 0)
    for offset in range(OFFSETS):
        picks = [
            (column == send_list[0, offset, 0, slot]).astype(jnp.float32) for slot in range(CAP)
        ]
        chosen[offset * 64 : (offset + 1) * 64] = jnp.concatenate(picks, axis=0).astype(jnp.bfloat16)
    for copy in halo:
        copy.wait()

    has_left = (me_x > 0).astype(jnp.float32)
    has_right = (me_x < n_server - 1).astype(jnp.float32)
    has_up = (me_y > 0).astype(jnp.float32)
    has_down = (me_y < n_mp - 1).astype(jnp.float32)
    top, low = PAD, PAD + HALO + CY
    for which, start, there in ((1, top, has_up), (0, low, has_down)):
        packet = edge_in[which].astype(jnp.float32) * there
        for f in range(FIELDS):
            cells[f, 0, start : start + HALO] = packet[f * HALO : (f + 1) * HALO]
    for right, left, start, count, there in (
        (side_in.at[0], side_in.at[1], PAD + HALO, CY, 1.0),
        (corner_in.at[2], corner_in.at[3], top, HALO, has_up),
        (corner_in.at[0], corner_in.at[1], low, HALO, has_down),
    ):
        packet_right = right[...].astype(jnp.float32) * (has_right * there)
        packet_left = left[...].astype(jnp.float32) * (has_left * there)
        spot = lax.broadcasted_iota(jnp.int32, (count, CX), 1)
        for i in range(3):
            from_right = packet_right[i * count : (i + 1) * count]
            from_left = packet_left[i * count : (i + 1) * count]
            for k in range(3):
                inside = (spot >= 40 * k) & (spot < 40 * k + 40)
                cells[3 * k + i, 1, start : start + count] = rolled(
                    jnp.where(inside, from_right, from_left), -40 * k
                )
    field_rows[6 * CY : 7 * CY] = mask[...].astype(jnp.bfloat16)
    field_rows[7 * CY : 8 * CY] = jnp.zeros((CY, CX), jnp.bfloat16)
    for part in range(2):
        moist[part] = jnp.where(cells[6, part] > 0.0, KEEP_V, 0.0)

    def ring(pair, step, first, last):
        a, b = (pltpu.roll(x, step % CX, 1) for x in pair)
        return (jnp.where(first, b, a), jnp.where(first, a, b)) if step == 1 else (jnp.where(last, b, a), jnp.where(last, a, b))

    def across(pair, first, last):
        before = ring(pair, 1, first, last)
        after = ring(pair, -1, first, last)
        return [y - x for x, y in zip(before, after)]

    def stresses(start, count, keep_pressure):
        spot = lax.broadcasted_iota(jnp.int32, (count, CX), 1)
        first, last = spot == 0, spot == CX - 1
        here, above, below = (pl.ds(start + d, count) for d in (0, -1, 1))
        u_x = across([cells[0, p, here] for p in range(2)], first, last)
        v_x = across([cells[1, p, here] for p in range(2)], first, last)
        for p in range(2):
            u_y = cells[0, p, below] - cells[0, p, above]
            v_y = cells[1, p, below] - cells[1, p, above]
            div, ten, shear = u_x[p] + v_y, u_x[p] - v_y, u_y + v_x[p]
            square = jnp.maximum(div * div + 0.25 * (ten * ten + shear * shear), TINY)
            deform = square * lax.rsqrt(square)
            bottom = deform + 1.0
            inverse = pl.reciprocal(bottom, approx=True)
            inverse = inverse * (2.0 - bottom * inverse)
            zeta = cells[5, p, here] * inverse
            one = zeta * (div - deform)
            two = (zeta * 0.25) * ten
            cells[2, p, here] = KEEP_S * cells[2, p, here] + (one + two)
            cells[3, p, here] = KEEP_S * cells[3, p, here] + (one - two)
            cells[4, p, here] = KEEP_S * cells[4, p, here] + (zeta * 0.5) * shear
            if keep_pressure and p == 0:
                pressure[pl.ds(start - PAD - HALO, count)] = zeta * deform * (1.0 / LOAD_SCALE)

    def velocities(start, count):
        spot = lax.broadcasted_iota(jnp.int32, (count, CX), 1)
        first, last = spot == 0, spot == CX - 1
        here, above, below = (pl.ds(start + d, count) for d in (0, -1, 1))
        p_x = across([cells[2, p, here] for p in range(2)], first, last)
        s_x = across([cells[4, p, here] for p in range(2)], first, last)
        for p in range(2):
            s_y = cells[4, p, below] - cells[4, p, above]
            m_y = cells[3, p, below] - cells[3, p, above]
            drag, keep = cells[6, p, here], moist[p, here]
            cells[0, p, here] = keep * cells[0, p, here] + ((p_x[p] + s_y) * drag + cells[7, p, here])
            cells[1, p, here] = keep * cells[1, p, here] + ((s_x[p] + m_y) * drag + cells[8, p, here])

    def subcycle(begin, end, inner, final=False):
        inside = range(HALO, HALO + CY, 8)
        for start in range(begin, end, 8):
            stresses(PAD + start, 8, final and start in inside)
        for start in range(begin + inner, end - inner, 8):
            velocities(PAD + start, 8)

    for stage in range(ITERS // 4):
        begin, end = 8 * stage, ROWS - 8 * stage

        def three(step, carry, begin=begin, end=end):
            subcycle(begin, end, 0)
            return carry

        lax.fori_loop(0, 3, three, 0)
        subcycle(begin, end, 8, stage == ITERS // 4 - 1)

    tile = slice(PAD + HALO, PAD + HALO + CY)
    plus, minus = cells[2, 0, tile], cells[3, 0, tile]
    results = (
        cells[0, 0, tile],
        cells[1, 0, tile],
        0.5 * (plus + minus),
        0.5 * (plus - minus),
        0.5 * cells[4, 0, tile],
    )
    for f, value in enumerate(results):
        state[f] = value
        field_rows[f * CY : (f + 1) * CY] = value.astype(jnp.bfloat16)
    field_rows[5 * CY : 6 * CY] = pressure[...].astype(jnp.bfloat16)
    state_store = pltpu.make_async_copy(state, state_hbm, state_sem)
    state_store.start()

    rows_copies = []
    for order, offset in enumerate((0, 1, 3, 4, 2)):
        packet = jnp.dot(
            chosen[offset * 64 : (offset + 1) * 64], field_rows[...], preferred_element_type=jnp.float32
        )
        if offset == 2:
            rows_all[offset * CAP : (offset + 1) * CAP] = packet.reshape(CAP, 8, CX)
            continue
        rows_out[order] = packet.astype(jnp.bfloat16)
        copy = pltpu.make_async_remote_copy(
            src_ref=rows_out.at[order],
            dst_ref=rows_in.at[order],
            send_sem=rows_send.at[order],
            recv_sem=rows_recv.at[order],
            device_id=device(offset - 2, 0),
            device_id_type=MESH,
        )
        copy.start()
        rows_copies.append((order, offset, copy))
    weight_load.wait()
    for order, offset, copy in rows_copies:
        copy.wait()
        rows_all[offset * CAP : (offset + 1) * CAP] = rows_in[order].astype(jnp.float32).reshape(CAP, 8, CX)

    for block in range(BLOCKS):
        total = jnp.zeros((8, CX), jnp.float32)
        for cross in range(CROSS):
            source = rows_all[block_index[0, 0, cross, block]].astype(jnp.bfloat16)
            total += jnp.dot(source, weights[0, 0, block, cross], preferred_element_type=jnp.float32)
        blocks_done[block] = total / jnp.maximum(total[6:7], FRAC_FLOOR)

    def for_span(span):
        found = jnp.zeros((8, CX), jnp.float32)
        for block in range(BLOCKS):
            found = jnp.where(span_slot[0, 0, block] == span, blocks_done[block], found)
        return found

    span_copies = []
    for hop in range(1, n_server):
        target = lax.rem(me_x + hop, n_server)
        spans_out[hop] = for_span(target)
        copy = pltpu.make_async_remote_copy(
            src_ref=spans_out.at[hop],
            dst_ref=spans_in.at[pl.ds(pl.multiple_of(me_x * 8, 8), 8)],
            send_sem=spans_send.at[hop],
            recv_sem=spans_recv.at[hop],
            device_id=(me_y, target),
            device_id_type=MESH,
        )
        copy.start()
        span_copies.append(copy)
    spans_in[pl.ds(pl.multiple_of(me_x * 8, 8), 8)] = for_span(me_x)
    for copy in span_copies:
        copy.wait()
    for f in range(6):
        written_ref[0, 0, f] = spans_in[pl.ds(f, n_server, stride=8)]
    state_store.wait()


def solution(mesh):
    n_mp, n_server = mesh.shape["mp"], mesh.shape["server"]
    placed = (
        P(None, "mp", "server"),
        P(None, "mp", "server"),
        P(None, "mp", "server"),
        P("mp", "server"),
        P("mp", "server"),
        P("mp", "server"),
        P("mp", "server", None, None),
        P("mp", "server", None, None),
        P("mp", "server", None),
        P("mp", "server", None, None, None, None),
    )
    f32, bf16 = jnp.float32, jnp.bfloat16
    far = pl.BlockSpec(memory_space=pltpu.HBM)

    def body(*arguments):
        arguments = list(arguments)
        arguments[6] = jnp.transpose(arguments[6], (0, 2, 1, 3))
        arguments[7] = jnp.transpose(arguments[7], (0, 1, 3, 2))
        return pl.pallas_call(
            functools.partial(kernel, n_mp, n_server),
            out_shape=(
                jax.ShapeDtypeStruct((5, CY, CX), f32),
                jax.ShapeDtypeStruct((1, 1, 6, 8, CX), f32),
            ),
            in_specs=[far] * 10,
            out_specs=(far, pl.BlockSpec(memory_space=pltpu.VMEM)),
            scratch_shapes=[
                pltpu.VMEM((2, CY, CX), f32),
                pltpu.VMEM((3, CY, CX), f32),
                pltpu.VMEM((2, CY, CX), f32),
                pltpu.VMEM((CY, CX), f32),
                pltpu.VMEM((CY, CX), f32),
                pltpu.VMEM((CY, CX), jnp.int32),
                pltpu.SMEM((1, OFFSETS, 1, CAP), jnp.int32),
                pltpu.SMEM((1, 1, CROSS, BLOCKS), jnp.int32),
                pltpu.SMEM((1, 1, BLOCKS), jnp.int32),
                pltpu.VMEM((1, 1, BLOCKS, CROSS, CX, CX), bf16),
                pltpu.VMEM((5, CY, CX), f32),
                pltpu.VMEM((FIELDS, 2, ROWS + 2 * PAD, CX), f32),
                pltpu.VMEM((2, ROWS + 2 * PAD, CX), f32),
                pltpu.VMEM((OFFSETS * 64, 8 * CY), bf16),
                pltpu.VMEM((CY, CX), f32),
                pltpu.VMEM((2, SIDE_ROWS, CX), bf16),
                pltpu.VMEM((2, EDGE_ROWS, CX), bf16),
                pltpu.VMEM((4, CORNER_ROWS, CX), bf16),
                pltpu.VMEM((2, SIDE_ROWS, CX), bf16),
                pltpu.VMEM((2, EDGE_ROWS, CX), bf16),
                pltpu.VMEM((4, CORNER_ROWS, CX), bf16),
                pltpu.VMEM((8 * CY, CX), bf16),
                pltpu.VMEM((4, 64, CX), bf16),
                pltpu.VMEM((4, 64, CX), bf16),
                pltpu.VMEM((OFFSETS * CAP, 8, CX), f32),
                pltpu.VMEM((BLOCKS, 8, CX), f32),
                pltpu.VMEM((8, 8, CX), f32),
                pltpu.VMEM((64, CX), f32),
                pltpu.SemaphoreType.DMA((9,)),
                pltpu.SemaphoreType.DMA,
                pltpu.SemaphoreType.DMA,
                pltpu.SemaphoreType.DMA((8,)),
                pltpu.SemaphoreType.DMA((8,)),
                pltpu.SemaphoreType.DMA((4,)),
                pltpu.SemaphoreType.DMA((4,)),
                pltpu.SemaphoreType.DMA((8,)),
                pltpu.SemaphoreType.DMA((8,)),
            ],
            compiler_params=pltpu.CompilerParams(
                collective_id=0, has_side_effects=True, vmem_limit_bytes=60 << 20
            ),
            name="ice",
        )(*arguments)

    return jax.shard_map(
        body,
        mesh=mesh,
        in_specs=placed,
        out_specs=(P(None, "mp", "server"), P("mp", "server", None, None, None)),
        check_vma=False,
    )
```

```python
import functools

import jax
import jax.numpy as jnp
from jax import lax
from jax.experimental import pallas as pl
from jax.experimental.pallas import tpu as pltpu
from jax.sharding import PartitionSpec as P

MESH = pl.DeviceIdType.MESH

CY, CX = 64, 128
ITERS = 20
HALO = 2 * ITERS
ROWS = CY + 2 * HALO
PAD = 8
FIELDS = 9
CAP, OFFSETS, BLOCKS, CROSS = 8, 5, 8, 4

RELAXATION = 0.1
STEP_SIZE = 0.3
DRAG_RATE = 1.0
FRAC_FLOOR = 0.3
KEEP_S = 1.0 / (1.0 + RELAXATION)
KEEP_V = 1.0 / (1.0 + STEP_SIZE * DRAG_RATE)
LOAD_SCALE = RELAXATION * 0.5 * KEEP_S
FORCE_SCALE = STEP_SIZE * KEEP_V * 0.25
WIND_SCALE = STEP_SIZE * KEEP_V
TINY = 1e-30

OWN_LANE = HALO // 2
RIGHT_LANE = (HALO + CX) // 2
SIDE_ROWS = 3 * CY
CORNER_ROWS = 80
EDGE_ROWS = 368
WIDTHS = (40, 32, 24, 16, 8)
STARTS = (0, 40, 72, 96, 112)
PLACE, BACK, SIDE, CORNER = 0, 256, 384, 1152

SPATIAL = ((0, -1), (0, 1), (-1, 0), (1, 0), (-1, -1), (-1, 1), (1, -1), (1, 1))
AROUND = SPATIAL + ((-2, 0), (2, 0)) + tuple((0, k) for k in range(2, 7))


def ones_where(condition):
    return jnp.where(condition, 1.0, 0.0).astype(jnp.bfloat16)


def fill_packing(packing):
    row = lax.broadcasted_iota(jnp.int32, (CX, CX), 0)
    shift = lax.broadcasted_iota(jnp.int32, (CX, CX), 1) - row
    slots = [(HALO, HALO * k) for k in range(3)] + list(zip(WIDTHS, STARTS))
    for i, (width, start) in enumerate(slots):
        rows = slice(i * CX, (i + 1) * CX)
        packing[rows, :CX] = ones_where((shift == start) & (row < width))
        packing[rows, CX:] = ones_where((shift == start - CX + width) & (row >= CX - width))


def fill_placing(placing):
    row = lax.broadcasted_iota(jnp.int32, (CX, CX), 0)
    column = lax.broadcasted_iota(jnp.int32, (CX, CX), 1)
    forth, back = 2 * column - row, 2 * row - column
    slots = [(SIDE + 2 * CX * k, HALO, HALO * k, 0) for k in range(3)]
    slots += [(CORNER + 2 * CX * g, WIDTHS[g], STARTS[g], 4 * g) for g in range(5)]
    for odd in range(2):
        own = ones_where(forth == HALO - odd)
        for half in range(2):
            placing[half * CX : (half + 1) * CX, PLACE + odd * CX : PLACE + (odd + 1) * CX] = own
        placing[odd * CX : (odd + 1) * CX, BACK:SIDE] = ones_where(back == HALO - odd)
        for at, width, start, lane in slots:
            columns = slice(at + odd * CX, at + (odd + 1) * CX)
            for half, first in enumerate((lane, RIGHT_LANE)):
                inside = (column >= first) & (column < first + width // 2)
                placing[half * CX : (half + 1) * CX, columns] = ones_where((forth == 2 * first - start - odd) & inside)


def split(x):
    high = x.astype(jnp.bfloat16)
    return high, (x - high.astype(jnp.float32)).astype(jnp.bfloat16)


def picked(x, matrix):
    return jnp.dot(x, matrix, preferred_element_type=jnp.float32)


def kernel(
    n_mp,
    n_server,
    vel_hbm,
    stress_hbm,
    wind_hbm,
    strength_hbm,
    mass_hbm,
    mask_hbm,
    send_list_hbm,
    block_index_hbm,
    span_slot_hbm,
    weights_hbm,
    state_ref,
    written_ref,
    vel,
    stress,
    wind,
    strength,
    mass,
    mask,
    send_list,
    block_index,
    span_slot,
    weights,
    packing,
    placing,
    cells,
    moist,
    chosen,
    pressure,
    side_out,
    edge_out,
    corner_out,
    side_in,
    edge_in,
    corner_in,
    field_rows,
    rows_out,
    rows_in,
    rows_all,
    blocks_done,
    spans_out,
    spans_in,
    in_sem,
    weight_sem,
    halo_send,
    halo_recv,
    rows_send,
    rows_recv,
    spans_send,
    spans_recv,
):
    me_y, me_x = lax.axis_index("mp"), lax.axis_index("server")

    def device(dy, dx):
        return (lax.rem(me_y + dy + n_mp, n_mp), lax.rem(me_x + dx + n_server, n_server))

    barrier = pltpu.get_barrier_semaphore()
    for dy, dx in AROUND:
        pl.semaphore_signal(barrier, inc=1, device_id=device(dy, dx), device_id_type=MESH)

    loads = [
        pltpu.make_async_copy(source, target, in_sem.at[i])
        for i, (source, target) in enumerate(
            (
                (vel_hbm, vel),
                (stress_hbm, stress),
                (wind_hbm, wind),
                (strength_hbm, strength),
                (mass_hbm, mass),
                (mask_hbm, mask),
                (send_list_hbm, send_list),
                (block_index_hbm, block_index),
                (span_slot_hbm, span_slot),
            )
        )
    ]
    for load in loads:
        load.start()
    weight_load = pltpu.make_async_copy(weights_hbm, weights, weight_sem)
    weight_load.start()
    fill_packing(packing)
    for load in loads[:6]:
        load.wait()

    ice = mask[...].astype(jnp.float32)
    per_mass = ice / mass[...]
    own = [
        vel[0],
        vel[1],
        stress[0] + stress[1],
        stress[0] - stress[1],
        stress[2] * 2.0,
        strength[...] * ice * LOAD_SCALE,
        per_mass * FORCE_SCALE,
        wind[0] * per_mass * WIND_SCALE,
        wind[1] * per_mass * WIND_SCALE,
    ]
    spare = jnp.zeros((8, CX), jnp.float32)
    edge_out[0] = jnp.concatenate([x[:HALO] for x in own] + [spare], axis=0).astype(jnp.bfloat16)
    edge_out[1] = jnp.concatenate([x[CY - HALO :] for x in own] + [spare], axis=0).astype(jnp.bfloat16)
    halo = [
        pltpu.make_async_remote_copy(
            src_ref=source,
            dst_ref=target,
            send_sem=halo_send.at[i],
            recv_sem=halo_recv.at[i],
            device_id=device(*SPATIAL[i]),
            device_id_type=MESH,
        )
        for i, (source, target) in enumerate(
            [(side_out.at[i], side_in.at[i]) for i in range(2)]
            + [(edge_out.at[i], edge_in.at[i]) for i in range(2)]
            + [(corner_out.at[i], corner_in.at[i]) for i in range(4)]
        )
    ]
    pl.semaphore_wait(barrier, len(AROUND))
    for i in (2, 3):
        halo[i].start()

    highs = [split(x) for x in own]
    sides = jnp.concatenate(
        [jnp.concatenate([highs[3 * k + i][0] for k in range(3)], axis=1) for i in range(3)], axis=0
    )
    packets = picked(sides, packing[: 3 * CX]).astype(jnp.bfloat16)
    for i in range(2):
        side_out[i] = packets[:, i * CX : (i + 1) * CX]
        halo[i].start()
    ends = []
    for edge in range(2):
        groups = [
            jnp.concatenate([x[8 * g : 8 * g + 8] if edge == 0 else x[CY - 8 - 8 * g : CY - 8 * g] for x in own], axis=0)
            for g in range(5)
        ]
        ends.append(jnp.concatenate([jnp.concatenate([x, spare], axis=0) for x in groups], axis=1))
    corners = picked(jnp.concatenate(ends, axis=0).astype(jnp.bfloat16), packing[3 * CX :]).astype(jnp.bfloat16)
    for i in range(4):
        corner_out[i] = corners[CORNER_ROWS * (i // 2) : CORNER_ROWS * (i // 2 + 1), CX * (i % 2) : CX * (i % 2 + 1)]
        halo[4 + i].start()

    for f in range(FIELDS):
        for part in range(2):
            cells[f, part, 0:PAD] = spare
            cells[f, part, PAD + ROWS : PAD + ROWS + PAD] = spare
    fill_placing(placing)
    for f in range(FIELDS):
        placed = picked(jnp.concatenate(highs[f], axis=1), placing[:, PLACE:BACK])
        for part in range(2):
            cells[f, part, PAD + HALO : PAD + HALO + CY] = placed[:, part * CX : (part + 1) * CX]

    for load in loads[6:]:
        load.wait()
    column = lax.broadcasted_iota(jnp.int32, (8, 8 * CY), 1) - CY * lax.broadcasted_iota(jnp.int32, (8, 8 * CY), 0)
    for offset in range(OFFSETS):
        picks = [
            (column == send_list[0, offset, 0, slot]).astype(jnp.float32) for slot in range(CAP)
        ]
        chosen[offset * 64 : (offset + 1) * 64] = jnp.concatenate(picks, axis=0).astype(jnp.bfloat16)
    has_left = (me_x > 0).astype(jnp.float32)
    has_right = (me_x < n_server - 1).astype(jnp.float32)
    has_up = (me_y > 0).astype(jnp.float32)
    has_down = (me_y < n_mp - 1).astype(jnp.float32)

    def kept(ref, there):
        return (ref[...].astype(jnp.float32) * there).astype(jnp.bfloat16)

    top, low = PAD, PAD + HALO + CY
    halo[0].wait_recv()
    halo[1].wait_recv()
    beside = jnp.concatenate([kept(side_in.at[1], has_left), kept(side_in.at[0], has_right)], axis=1)
    for k in range(3):
        found = picked(beside, placing[:, SIDE + 2 * CX * k : SIDE + 2 * CX * (k + 1)])
        for i in range(3):
            for part in range(2):
                cells[3 * k + i, part, PAD + HALO : low] += found[i * CY : (i + 1) * CY, part * CX : (part + 1) * CX]
    for which, start, there in ((1, top, has_up), (0, low, has_down)):
        halo[2 + which].wait_recv()
        found = picked(kept(edge_in.at[which], there), placing[:CX, PLACE:BACK])
        for f in range(FIELDS):
            for part in range(2):
                cells[f, part, start : start + HALO] = found[f * HALO : (f + 1) * HALO, part * CX : (part + 1) * CX]
    for copy in halo[4:]:
        copy.wait_recv()
    for from_left, from_right, start, there in ((3, 2, top, has_up), (1, 0, low, has_down)):
        beyond = jnp.concatenate(
            [kept(corner_in.at[from_left], has_left * there), kept(corner_in.at[from_right], has_right * there)], axis=1
        )
        for g in range(5):
            found = picked(beyond, placing[:, CORNER + 2 * CX * g : CORNER + 2 * CX * (g + 1)])
            at = start + (HALO - 8 - 8 * g if start == top else 8 * g)
            for f in range(FIELDS):
                for part in range(2):
                    cells[f, part, at : at + 8] += found[f * 8 : (f + 1) * 8, part * CX : (part + 1) * CX]
    field_rows[6 * CY : 7 * CY] = mask[...].astype(jnp.bfloat16)
    field_rows[7 * CY : 8 * CY] = jnp.zeros((CY, CX), jnp.bfloat16)
    for part in range(2):
        moist[part] = jnp.where(cells[6, part] > 0.0, KEEP_V, 0.0)

    def across(even, odd):
        return odd - pltpu.roll(odd, 1, 1), pltpu.roll(even, CX - 1, 1) - even

    def stresses(start, count, keep_pressure):
        here, above, below = (pl.ds(start + d, count) for d in (0, -1, 1))
        u_x = across(*(cells[0, p, here] for p in range(2)))
        v_x = across(*(cells[1, p, here] for p in range(2)))
        for p in range(2):
            u_y = cells[0, p, below] - cells[0, p, above]
            v_y = cells[1, p, below] - cells[1, p, above]
            div, ten, shear = u_x[p] + v_y, u_x[p] - v_y, u_y + v_x[p]
            square = jnp.maximum(div * div + 0.25 * (ten * ten + shear * shear), TINY)
            deform = square * lax.rsqrt(square)
            bottom = deform + 1.0
            inverse = pl.reciprocal(bottom, approx=True)
            zeta = cells[5, p, here] * inverse
            one = zeta * (div - deform)
            two = (zeta * 0.25) * ten
            cells[2, p, here] = KEEP_S * cells[2, p, here] + (one + two)
            cells[3, p, here] = KEEP_S * cells[3, p, here] + (one - two)
            cells[4, p, here] = KEEP_S * cells[4, p, here] + (zeta * 0.5) * shear
            if keep_pressure:
                pressure[p, pl.ds(start - PAD - HALO, count)] = zeta * deform * (1.0 / LOAD_SCALE)

    def velocities(start, count):
        here, above, below = (pl.ds(start + d, count) for d in (0, -1, 1))
        p_x = across(*(cells[2, p, here] for p in range(2)))
        s_x = across(*(cells[4, p, here] for p in range(2)))
        for p in range(2):
            s_y = cells[4, p, below] - cells[4, p, above]
            m_y = cells[3, p, below] - cells[3, p, above]
            drag, keep = cells[6, p, here], moist[p, here]
            cells[0, p, here] = keep * cells[0, p, here] + ((p_x[p] + s_y) * drag + cells[7, p, here])
            cells[1, p, here] = keep * cells[1, p, here] + ((s_x[p] + m_y) * drag + cells[8, p, here])

    wave = []
    for step in range(ITERS):
        first, last, inner = step // 4, ROWS // 8 - step // 4, int(step % 4 == 3)
        wave += [(6 * step + group, 1, step, group) for group in range(first, last)]
        wave += [(6 * step + group + 3, 0, step, group) for group in range(first + inner, last - inner)]
    for _, is_stress, step, group in sorted(wave):
        if is_stress:
            stresses(PAD + 8 * group, 8, step == ITERS - 1 and HALO <= 8 * group < HALO + CY)
        else:
            velocities(PAD + 8 * group, 8)

    tile = slice(PAD + HALO, PAD + HALO + CY)

    def results(part):
        plus, minus = cells[2, part, tile], cells[3, part, tile]
        yield cells[0, part, tile]
        yield cells[1, part, tile]
        yield 0.5 * (plus + minus)
        yield 0.5 * (plus - minus)
        yield 0.5 * cells[4, part, tile]

    back = placing[:, BACK:SIDE]
    rests = []
    for f, pair in enumerate(zip(results(0), results(1))):
        high, rest = zip(*(split(x) for x in pair))
        rests.append(rest)
        rounded = picked(jnp.concatenate(high, axis=1), back)
        state_ref[f] = rounded
        field_rows[f * CY : (f + 1) * CY] = rounded.astype(jnp.bfloat16)
    ends = jnp.concatenate([pressure[p].astype(jnp.bfloat16) for p in range(2)], axis=1)
    field_rows[5 * CY : 6 * CY] = picked(ends, back).astype(jnp.bfloat16)

    rows_copies = []
    for order, offset in enumerate((0, 1, 3, 4, 2)):
        packet = jnp.dot(
            chosen[offset * 64 : (offset + 1) * 64], field_rows[...], preferred_element_type=jnp.float32
        )
        if offset == 2:
            rows_all[offset * CAP : (offset + 1) * CAP] = packet.reshape(CAP, 8, CX)
            continue
        rows_out[order] = packet.astype(jnp.bfloat16)
        copy = pltpu.make_async_remote_copy(
            src_ref=rows_out.at[order],
            dst_ref=rows_in.at[order],
            send_sem=rows_send.at[order],
            recv_sem=rows_recv.at[order],
            device_id=device(offset - 2, 0),
            device_id_type=MESH,
        )
        copy.start()
        rows_copies.append((order, offset, copy))
    for f, rest in enumerate(rests):
        state_ref[f] += picked(jnp.concatenate(rest, axis=1), back)
    weight_load.wait()
    for order, offset, copy in rows_copies:
        copy.wait_recv()
        rows_all[offset * CAP : (offset + 1) * CAP] = rows_in[order].astype(jnp.float32).reshape(CAP, 8, CX)

    for block in range(BLOCKS):
        total = jnp.zeros((8, CX), jnp.float32)
        for cross in range(CROSS):
            source = rows_all[block_index[0, 0, cross, block]].astype(jnp.bfloat16)
            total += jnp.dot(source, weights[0, 0, block, cross], preferred_element_type=jnp.float32)
        blocks_done[block] = total / jnp.maximum(total[6:7], FRAC_FLOOR)

    def for_span(span):
        found = jnp.zeros((8, CX), jnp.float32)
        for block in range(BLOCKS):
            found = jnp.where(span_slot[0, 0, block] == span, blocks_done[block], found)
        return found

    span_copies = []
    for hop in range(1, n_server):
        target = lax.rem(me_x + hop, n_server)
        spans_out[hop] = for_span(target)
        copy = pltpu.make_async_remote_copy(
            src_ref=spans_out.at[hop],
            dst_ref=spans_in.at[pl.ds(pl.multiple_of(me_x * 8, 8), 8)],
            send_sem=spans_send.at[hop],
            recv_sem=spans_recv.at[hop],
            device_id=(me_y, target),
            device_id_type=MESH,
        )
        copy.start()
        span_copies.append(copy)
    spans_in[pl.ds(pl.multiple_of(me_x * 8, 8), 8)] = for_span(me_x)
    for copy in span_copies:
        copy.wait_recv()
    for f in range(6):
        written_ref[0, 0, f] = spans_in[pl.ds(f, n_server, stride=8)]
    for copy in halo + [copy for _, _, copy in rows_copies] + span_copies:
        copy.wait_send()


def solution(mesh):
    n_mp, n_server = mesh.shape["mp"], mesh.shape["server"]
    placed = (
        P(None, "mp", "server"),
        P(None, "mp", "server"),
        P(None, "mp", "server"),
        P("mp", "server"),
        P("mp", "server"),
        P("mp", "server"),
        P("mp", "server", None, None),
        P("mp", "server", None, None),
        P("mp", "server", None),
        P("mp", "server", None, None, None, None),
    )
    f32, bf16 = jnp.float32, jnp.bfloat16
    far = pl.BlockSpec(memory_space=pltpu.HBM)

    def body(*arguments):
        arguments = list(arguments)
        arguments[6] = jnp.transpose(arguments[6], (0, 2, 1, 3))
        arguments[7] = jnp.transpose(arguments[7], (0, 1, 3, 2))
        return pl.pallas_call(
            functools.partial(kernel, n_mp, n_server),
            out_shape=(
                pltpu.VMEM((5, CY, CX), f32),
                pltpu.VMEM((1, 1, 6, 8, CX), f32),
            ),
            in_specs=[far] * 10,
            out_specs=[pl.BlockSpec(memory_space=pltpu.VMEM)] * 2,
            scratch_shapes=[
                pltpu.VMEM((2, CY, CX), f32),
                pltpu.VMEM((3, CY, CX), f32),
                pltpu.VMEM((2, CY, CX), f32),
                pltpu.VMEM((CY, CX), f32),
                pltpu.VMEM((CY, CX), f32),
                pltpu.VMEM((CY, CX), jnp.int32),
                pltpu.SMEM((1, OFFSETS, 1, CAP), jnp.int32),
                pltpu.SMEM((1, 1, CROSS, BLOCKS), jnp.int32),
                pltpu.SMEM((1, 1, BLOCKS), jnp.int32),
                pltpu.VMEM((1, 1, BLOCKS, CROSS, CX, CX), bf16),
                pltpu.VMEM((8 * CX, 2 * CX), bf16),
                pltpu.VMEM((2 * CX, CORNER + 10 * CX), bf16),
                pltpu.VMEM((FIELDS, 2, ROWS + 2 * PAD, CX), f32),
                pltpu.VMEM((2, ROWS + 2 * PAD, CX), f32),
                pltpu.VMEM((OFFSETS * 64, 8 * CY), bf16),
                pltpu.VMEM((2, CY, CX), f32),
                pltpu.VMEM((2, SIDE_ROWS, CX), bf16),
                pltpu.VMEM((2, EDGE_ROWS, CX), bf16),
                pltpu.VMEM((4, CORNER_ROWS, CX), bf16),
                pltpu.VMEM((2, SIDE_ROWS, CX), bf16),
                pltpu.VMEM((2, EDGE_ROWS, CX), bf16),
                pltpu.VMEM((4, CORNER_ROWS, CX), bf16),
                pltpu.VMEM((8 * CY, CX), bf16),
                pltpu.VMEM((4, 64, CX), bf16),
                pltpu.VMEM((4, 64, CX), bf16),
                pltpu.VMEM((OFFSETS * CAP, 8, CX), f32),
                pltpu.VMEM((BLOCKS, 8, CX), f32),
                pltpu.VMEM((8, 8, CX), f32),
                pltpu.VMEM((64, CX), f32),
                pltpu.SemaphoreType.DMA((9,)),
                pltpu.SemaphoreType.DMA,
                pltpu.SemaphoreType.DMA((8,)),
                pltpu.SemaphoreType.DMA((8,)),
                pltpu.SemaphoreType.DMA((4,)),
                pltpu.SemaphoreType.DMA((4,)),
                pltpu.SemaphoreType.DMA((8,)),
                pltpu.SemaphoreType.DMA((8,)),
            ],
            compiler_params=pltpu.CompilerParams(
                collective_id=0, has_side_effects=True, vmem_limit_bytes=60 << 20
            ),
            name="ice",
        )(*arguments)

    return jax.shard_map(
        body,
        mesh=mesh,
        in_specs=placed,
        out_specs=(P(None, "mp", "server"), P("mp", "server", None, None, None)),
        check_vma=False,
    )
```

```python
import functools

import jax
import jax.numpy as jnp
from jax import lax
from jax.experimental import pallas as pl
from jax.experimental.pallas import tpu as pltpu
from jax.sharding import PartitionSpec as P

MESH = pl.DeviceIdType.MESH

CY, CX = 64, 128
ITERS = 20
HALO = 2 * ITERS
ROWS = CY + 2 * HALO
PAD = 8
FIELDS = 9
CAP, OFFSETS, BLOCKS, CROSS = 8, 5, 8, 4

RELAXATION = 0.1
STEP_SIZE = 0.3
DRAG_RATE = 1.0
FRAC_FLOOR = 0.3
KEEP_S = 1.0 / (1.0 + RELAXATION)
KEEP_V = 1.0 / (1.0 + STEP_SIZE * DRAG_RATE)
LOAD_SCALE = RELAXATION * 0.5 * KEEP_S
FORCE_SCALE = STEP_SIZE * KEEP_V * 0.25
WIND_SCALE = STEP_SIZE * KEEP_V
TINY = 1e-30

OWN_LANE = HALO // 2
RIGHT_LANE = (HALO + CX) // 2
SIDE_ROWS = 3 * CY
CORNER_ROWS = 80
EDGE_ROWS = 368
WIDTHS = (40, 32, 24, 16, 8)
STARTS = (0, 40, 72, 96, 112)
PLACE, BACK, SIDE, CORNER = 0, 256, 384, 1152

SPATIAL = ((0, -1), (0, 1), (-1, 0), (1, 0), (-1, -1), (-1, 1), (1, -1), (1, 1))
AROUND = SPATIAL + ((-2, 0), (2, 0)) + tuple((0, k) for k in range(2, 7))


def ones_where(condition):
    return jnp.where(condition, 1.0, 0.0).astype(jnp.bfloat16)


def fill_packing(packing):
    row = lax.broadcasted_iota(jnp.int32, (CX, CX), 0)
    shift = lax.broadcasted_iota(jnp.int32, (CX, CX), 1) - row
    slots = [(HALO, HALO * k) for k in range(3)] + list(zip(WIDTHS, STARTS))
    for i, (width, start) in enumerate(slots):
        rows = slice(i * CX, (i + 1) * CX)
        packing[rows, :CX] = ones_where((shift == start) & (row < width))
        packing[rows, CX:] = ones_where((shift == start - CX + width) & (row >= CX - width))


def fill_placing(placing):
    row = lax.broadcasted_iota(jnp.int32, (CX, CX), 0)
    column = lax.broadcasted_iota(jnp.int32, (CX, CX), 1)
    forth, back = 2 * column - row, 2 * row - column
    slots = [(SIDE + 2 * CX * k, HALO, HALO * k, 0) for k in range(3)]
    slots += [(CORNER + 2 * CX * g, WIDTHS[g], STARTS[g], 4 * g) for g in range(5)]
    for odd in range(2):
        own = ones_where(forth == HALO - odd)
        for half in range(2):
            placing[half * CX : (half + 1) * CX, PLACE + odd * CX : PLACE + (odd + 1) * CX] = own
        placing[odd * CX : (odd + 1) * CX, BACK:SIDE] = ones_where(back == HALO - odd)
        for at, width, start, lane in slots:
            columns = slice(at + odd * CX, at + (odd + 1) * CX)
            for half, first in enumerate((lane, RIGHT_LANE)):
                inside = (column >= first) & (column < first + width // 2)
                placing[half * CX : (half + 1) * CX, columns] = ones_where((forth == 2 * first - start - odd) & inside)


def split(x):
    high = x.astype(jnp.bfloat16)
    return high, (x - high.astype(jnp.float32)).astype(jnp.bfloat16)


def picked(x, matrix):
    return jnp.dot(x, matrix, preferred_element_type=jnp.float32)


def kernel(
    n_mp,
    n_server,
    vel_hbm,
    stress_hbm,
    wind_hbm,
    strength_hbm,
    mass_hbm,
    mask_hbm,
    send_list_hbm,
    block_index_hbm,
    span_slot_hbm,
    weights_hbm,
    state_ref,
    written_ref,
    vel,
    stress,
    wind,
    strength,
    mass,
    mask,
    send_list,
    block_index,
    span_slot,
    weights,
    packing,
    placing,
    cells,
    moist,
    chosen,
    pressure,
    side_out,
    edge_out,
    corner_out,
    side_in,
    edge_in,
    corner_in,
    field_rows,
    rows_out,
    rows_in,
    rows_all,
    blocks_done,
    spans_out,
    spans_in,
    in_sem,
    weight_sem,
    halo_send,
    halo_recv,
    rows_send,
    rows_recv,
    spans_send,
    spans_recv,
):
    me_y, me_x = lax.axis_index("mp"), lax.axis_index("server")

    def device(dy, dx):
        return (lax.rem(me_y + dy + n_mp, n_mp), lax.rem(me_x + dx + n_server, n_server))

    def inside(dy, dx):
        found = None
        for step, at, count in ((dy, me_y, n_mp), (dx, me_x, n_server)):
            if step:
                there = at >= -step if step < 0 else at < count - step
                found = there if found is None else found & there
        return found

    def where_inside(dy, dx, action):
        there = inside(dy, dx)
        action() if there is None else pl.when(there)(action)

    barrier = pltpu.get_barrier_semaphore()
    greeted = jnp.int32(0)
    for dy, dx in AROUND:
        where_inside(
            dy,
            0,
            lambda dy=dy, dx=dx: pl.semaphore_signal(
                barrier, inc=1, device_id=device(dy, dx), device_id_type=MESH
            ),
        )
        greeted = greeted + (1 if dy == 0 else inside(dy, 0).astype(jnp.int32))

    loads = [
        pltpu.make_async_copy(source, target, in_sem.at[i])
        for i, (source, target) in enumerate(
            (
                (vel_hbm, vel),
                (stress_hbm, stress),
                (wind_hbm, wind),
                (strength_hbm, strength),
                (mass_hbm, mass),
                (mask_hbm, mask),
                (send_list_hbm, send_list),
                (block_index_hbm, block_index),
                (span_slot_hbm, span_slot),
            )
        )
    ]
    for load in loads:
        load.start()
    weight_load = pltpu.make_async_copy(weights_hbm, weights, weight_sem)
    weight_load.start()
    fill_packing(packing)
    for load in loads[:6]:
        load.wait()

    ice = mask[...].astype(jnp.float32)
    per_mass = ice / mass[...]
    own = [
        vel[0],
        vel[1],
        stress[0] + stress[1],
        stress[0] - stress[1],
        stress[2] * 2.0,
        strength[...] * ice * LOAD_SCALE,
        per_mass * FORCE_SCALE,
        wind[0] * per_mass * WIND_SCALE,
        wind[1] * per_mass * WIND_SCALE,
    ]
    spare = jnp.zeros((8, CX), jnp.float32)
    edge_out[0] = jnp.concatenate([x[:HALO] for x in own] + [spare], axis=0).astype(jnp.bfloat16)
    edge_out[1] = jnp.concatenate([x[CY - HALO :] for x in own] + [spare], axis=0).astype(jnp.bfloat16)
    halo = [
        pltpu.make_async_remote_copy(
            src_ref=source,
            dst_ref=target,
            send_sem=halo_send.at[i],
            recv_sem=halo_recv.at[i],
            device_id=device(*SPATIAL[i]),
            device_id_type=MESH,
        )
        for i, (source, target) in enumerate(
            [(side_out.at[i], side_in.at[i]) for i in range(2)]
            + [(edge_out.at[i], edge_in.at[i]) for i in range(2)]
            + [(corner_out.at[i], corner_in.at[i]) for i in range(4)]
        )
    ]
    pl.semaphore_wait(barrier, greeted)

    def send_halo(i):
        where_inside(*SPATIAL[i], lambda: halo[i].start())

    def receive_halo(i):
        where_inside(*(-step for step in SPATIAL[i]), lambda: halo[i].wait_recv())

    for i in (2, 3):
        send_halo(i)

    highs = [split(x) for x in own]
    sides = jnp.concatenate(
        [jnp.concatenate([highs[3 * k + i][0] for k in range(3)], axis=1) for i in range(3)], axis=0
    )
    packets = picked(sides, packing[: 3 * CX]).astype(jnp.bfloat16)
    for i in range(2):
        side_out[i] = packets[:, i * CX : (i + 1) * CX]
        send_halo(i)
    ends = []
    for edge in range(2):
        groups = [
            jnp.concatenate([x[8 * g : 8 * g + 8] if edge == 0 else x[CY - 8 - 8 * g : CY - 8 * g] for x in own], axis=0)
            for g in range(5)
        ]
        ends.append(jnp.concatenate([jnp.concatenate([x, spare], axis=0) for x in groups], axis=1))
    corners = picked(jnp.concatenate(ends, axis=0).astype(jnp.bfloat16), packing[3 * CX :]).astype(jnp.bfloat16)
    for i in range(4):
        corner_out[i] = corners[CORNER_ROWS * (i // 2) : CORNER_ROWS * (i // 2 + 1), CX * (i % 2) : CX * (i % 2 + 1)]
        send_halo(4 + i)

    for f in range(FIELDS):
        for part in range(2):
            cells[f, part, 0:PAD] = spare
            cells[f, part, PAD + ROWS : PAD + ROWS + PAD] = spare
    fill_placing(placing)
    for f in range(FIELDS):
        placed = picked(jnp.concatenate(highs[f], axis=1), placing[:, PLACE:BACK])
        for part in range(2):
            cells[f, part, PAD + HALO : PAD + HALO + CY] = placed[:, part * CX : (part + 1) * CX]

    for load in loads[6:]:
        load.wait()
    column = lax.broadcasted_iota(jnp.int32, (8, 8 * CY), 1) - CY * lax.broadcasted_iota(jnp.int32, (8, 8 * CY), 0)
    for offset in range(OFFSETS):
        picks = [
            (column == send_list[0, offset, 0, slot]).astype(jnp.float32) for slot in range(CAP)
        ]
        chosen[offset * 64 : (offset + 1) * 64] = jnp.concatenate(picks, axis=0).astype(jnp.bfloat16)
    has_left, has_right = me_x > 0, me_x < n_server - 1
    has_up, has_down = me_y > 0, me_y < n_mp - 1

    def kept(ref, there):
        return jnp.where(there, ref[...].astype(jnp.float32), 0.0).astype(jnp.bfloat16)

    top, low = PAD, PAD + HALO + CY
    receive_halo(0)
    receive_halo(1)
    beside = jnp.concatenate([kept(side_in.at[1], has_left), kept(side_in.at[0], has_right)], axis=1)
    for k in range(3):
        found = picked(beside, placing[:, SIDE + 2 * CX * k : SIDE + 2 * CX * (k + 1)])
        for i in range(3):
            for part in range(2):
                cells[3 * k + i, part, PAD + HALO : low] += found[i * CY : (i + 1) * CY, part * CX : (part + 1) * CX]
    for which, start, there in ((1, top, has_up), (0, low, has_down)):
        receive_halo(2 + which)
        found = picked(kept(edge_in.at[which], there), placing[:CX, PLACE:BACK])
        for f in range(FIELDS):
            for part in range(2):
                cells[f, part, start : start + HALO] = found[f * HALO : (f + 1) * HALO, part * CX : (part + 1) * CX]
    for i in range(4, 8):
        receive_halo(i)
    for from_left, from_right, start, there in ((3, 2, top, has_up), (1, 0, low, has_down)):
        beyond = jnp.concatenate(
            [kept(corner_in.at[from_left], has_left & there), kept(corner_in.at[from_right], has_right & there)], axis=1
        )
        for g in range(5):
            found = picked(beyond, placing[:, CORNER + 2 * CX * g : CORNER + 2 * CX * (g + 1)])
            at = start + (HALO - 8 - 8 * g if start == top else 8 * g)
            for f in range(FIELDS):
                for part in range(2):
                    cells[f, part, at : at + 8] += found[f * 8 : (f + 1) * 8, part * CX : (part + 1) * CX]
    field_rows[6 * CY : 7 * CY] = mask[...].astype(jnp.bfloat16)
    field_rows[7 * CY : 8 * CY] = jnp.zeros((CY, CX), jnp.bfloat16)
    for part in range(2):
        moist[part] = jnp.where(cells[6, part] > 0.0, KEEP_V, 0.0)

    def across(even, odd):
        return odd - pltpu.roll(odd, 1, 1), pltpu.roll(even, CX - 1, 1) - even

    def stresses(start, count, keep_pressure):
        here, above, below = (pl.ds(start + d, count) for d in (0, -1, 1))
        u_x = across(*(cells[0, p, here] for p in range(2)))
        v_x = across(*(cells[1, p, here] for p in range(2)))
        for p in range(2):
            u_y = cells[0, p, below] - cells[0, p, above]
            v_y = cells[1, p, below] - cells[1, p, above]
            div, ten, shear = u_x[p] + v_y, u_x[p] - v_y, u_y + v_x[p]
            square = jnp.maximum(div * div + 0.25 * (ten * ten + shear * shear), TINY)
            deform = square * lax.rsqrt(square)
            bottom = deform + 1.0
            inverse = pl.reciprocal(bottom, approx=True)
            zeta = cells[5, p, here] * inverse
            one = zeta * (div - deform)
            two = (zeta * 0.25) * ten
            cells[2, p, here] = KEEP_S * cells[2, p, here] + (one + two)
            cells[3, p, here] = KEEP_S * cells[3, p, here] + (one - two)
            cells[4, p, here] = KEEP_S * cells[4, p, here] + (zeta * 0.5) * shear
            if keep_pressure:
                pressure[p, pl.ds(start - PAD - HALO, count)] = zeta * deform * (1.0 / LOAD_SCALE)

    def velocities(start, count):
        here, above, below = (pl.ds(start + d, count) for d in (0, -1, 1))
        p_x = across(*(cells[2, p, here] for p in range(2)))
        s_x = across(*(cells[4, p, here] for p in range(2)))
        for p in range(2):
            s_y = cells[4, p, below] - cells[4, p, above]
            m_y = cells[3, p, below] - cells[3, p, above]
            drag, keep = cells[6, p, here], moist[p, here]
            cells[0, p, here] = keep * cells[0, p, here] + ((p_x[p] + s_y) * drag + cells[7, p, here])
            cells[1, p, here] = keep * cells[1, p, here] + ((s_x[p] + m_y) * drag + cells[8, p, here])

    wave = []
    for step in range(ITERS):
        first, last, inner = step // 4, ROWS // 8 - step // 4, int(step % 4 == 3)
        wave += [(6 * step + group, 1, step, group) for group in range(first, last)]
        wave += [(6 * step + group + 3, 0, step, group) for group in range(first + inner, last - inner)]
    for _, is_stress, step, group in sorted(wave):
        if is_stress:
            stresses(PAD + 8 * group, 8, step == ITERS - 1 and HALO <= 8 * group < HALO + CY)
        else:
            velocities(PAD + 8 * group, 8)

    tile = slice(PAD + HALO, PAD + HALO + CY)

    def results(part):
        plus, minus = cells[2, part, tile], cells[3, part, tile]
        yield cells[0, part, tile]
        yield cells[1, part, tile]
        yield 0.5 * (plus + minus)
        yield 0.5 * (plus - minus)
        yield 0.5 * cells[4, part, tile]

    back = placing[:, BACK:SIDE]
    rests = []
    for f, pair in enumerate(zip(results(0), results(1))):
        high, rest = zip(*(split(x) for x in pair))
        rests.append(rest)
        rounded = picked(jnp.concatenate(high, axis=1), back)
        state_ref[f] = rounded
        field_rows[f * CY : (f + 1) * CY] = rounded.astype(jnp.bfloat16)
    ends = jnp.concatenate([pressure[p].astype(jnp.bfloat16) for p in range(2)], axis=1)
    field_rows[5 * CY : 6 * CY] = picked(ends, back).astype(jnp.bfloat16)

    rows_copies = []
    for order, offset in enumerate((0, 1, 3, 4, 2)):
        packet = jnp.dot(
            chosen[offset * 64 : (offset + 1) * 64], field_rows[...], preferred_element_type=jnp.float32
        )
        if offset == 2:
            rows_all[offset * CAP : (offset + 1) * CAP] = packet.reshape(CAP, 8, CX)
            continue
        rows_out[order] = packet.astype(jnp.bfloat16)
        copy = pltpu.make_async_remote_copy(
            src_ref=rows_out.at[order],
            dst_ref=rows_in.at[order],
            send_sem=rows_send.at[order],
            recv_sem=rows_recv.at[order],
            device_id=device(offset - 2, 0),
            device_id_type=MESH,
        )
        where_inside(offset - 2, 0, copy.start)
        rows_copies.append((order, offset, copy))
    for f, rest in enumerate(rests):
        state_ref[f] += picked(jnp.concatenate(rest, axis=1), back)
    weight_load.wait()
    for order, offset, copy in rows_copies:
        where_inside(2 - offset, 0, copy.wait_recv)
        rows_all[offset * CAP : (offset + 1) * CAP] = rows_in[order].astype(jnp.float32).reshape(CAP, 8, CX)

    for block in range(BLOCKS):
        source = jnp.concatenate(
            [rows_all[block_index[0, 0, cross, block]] for cross in range(CROSS)], axis=1
        ).astype(jnp.bfloat16)
        total = picked(source, weights[0, 0, block].reshape(CROSS * CX, CX))
        blocks_done[block] = total / jnp.maximum(total[6:7], FRAC_FLOOR)

    def for_span(span):
        found = jnp.zeros((8, CX), jnp.float32)
        for block in range(BLOCKS):
            found = jnp.where(span_slot[0, 0, block] == span, blocks_done[block], found)
        return found

    span_copies = []
    for hop in range(1, n_server):
        target = lax.rem(me_x + hop, n_server)
        spans_out[hop] = for_span(target)
        copy = pltpu.make_async_remote_copy(
            src_ref=spans_out.at[hop],
            dst_ref=spans_in.at[pl.ds(pl.multiple_of(me_x * 8, 8), 8)],
            send_sem=spans_send.at[hop],
            recv_sem=spans_recv.at[hop],
            device_id=(me_y, target),
            device_id_type=MESH,
        )
        copy.start()
        span_copies.append(copy)
    spans_in[pl.ds(pl.multiple_of(me_x * 8, 8), 8)] = for_span(me_x)
    for copy in span_copies:
        copy.wait_recv()
    for f in range(6):
        written_ref[0, 0, f] = spans_in[pl.ds(f, n_server, stride=8)]
    for i, copy in enumerate(halo):
        where_inside(*SPATIAL[i], copy.wait_send)
    for _, offset, copy in rows_copies:
        where_inside(offset - 2, 0, copy.wait_send)
    for copy in span_copies:
        copy.wait_send()


def solution(mesh):
    n_mp, n_server = mesh.shape["mp"], mesh.shape["server"]
    placed = (
        P(None, "mp", "server"),
        P(None, "mp", "server"),
        P(None, "mp", "server"),
        P("mp", "server"),
        P("mp", "server"),
        P("mp", "server"),
        P("mp", "server", None, None),
        P("mp", "server", None, None),
        P("mp", "server", None),
        P("mp", "server", None, None, None, None),
    )
    f32, bf16 = jnp.float32, jnp.bfloat16
    far = pl.BlockSpec(memory_space=pltpu.HBM)

    def body(*arguments):
        arguments = list(arguments)
        arguments[6] = jnp.transpose(arguments[6], (0, 2, 1, 3))
        arguments[7] = jnp.transpose(arguments[7], (0, 1, 3, 2))
        return pl.pallas_call(
            functools.partial(kernel, n_mp, n_server),
            out_shape=(
                pltpu.VMEM((5, CY, CX), f32),
                pltpu.VMEM((1, 1, 6, 8, CX), f32),
            ),
            in_specs=[far] * 10,
            out_specs=[pl.BlockSpec(memory_space=pltpu.VMEM)] * 2,
            scratch_shapes=[
                pltpu.VMEM((2, CY, CX), f32),
                pltpu.VMEM((3, CY, CX), f32),
                pltpu.VMEM((2, CY, CX), f32),
                pltpu.VMEM((CY, CX), f32),
                pltpu.VMEM((CY, CX), f32),
                pltpu.VMEM((CY, CX), jnp.int32),
                pltpu.SMEM((1, OFFSETS, 1, CAP), jnp.int32),
                pltpu.SMEM((1, 1, CROSS, BLOCKS), jnp.int32),
                pltpu.SMEM((1, 1, BLOCKS), jnp.int32),
                pltpu.VMEM((1, 1, BLOCKS, CROSS, CX, CX), bf16),
                pltpu.VMEM((8 * CX, 2 * CX), bf16),
                pltpu.VMEM((2 * CX, CORNER + 10 * CX), bf16),
                pltpu.VMEM((FIELDS, 2, ROWS + 2 * PAD, CX), f32),
                pltpu.VMEM((2, ROWS + 2 * PAD, CX), f32),
                pltpu.VMEM((OFFSETS * 64, 8 * CY), bf16),
                pltpu.VMEM((2, CY, CX), f32),
                pltpu.VMEM((2, SIDE_ROWS, CX), bf16),
                pltpu.VMEM((2, EDGE_ROWS, CX), bf16),
                pltpu.VMEM((4, CORNER_ROWS, CX), bf16),
                pltpu.VMEM((2, SIDE_ROWS, CX), bf16),
                pltpu.VMEM((2, EDGE_ROWS, CX), bf16),
                pltpu.VMEM((4, CORNER_ROWS, CX), bf16),
                pltpu.VMEM((8 * CY, CX), bf16),
                pltpu.VMEM((4, 64, CX), bf16),
                pltpu.VMEM((4, 64, CX), bf16),
                pltpu.VMEM((OFFSETS * CAP, 8, CX), f32),
                pltpu.VMEM((BLOCKS, 8, CX), f32),
                pltpu.VMEM((8, 8, CX), f32),
                pltpu.VMEM((64, CX), f32),
                pltpu.SemaphoreType.DMA((9,)),
                pltpu.SemaphoreType.DMA,
                pltpu.SemaphoreType.DMA((8,)),
                pltpu.SemaphoreType.DMA((8,)),
                pltpu.SemaphoreType.DMA((4,)),
                pltpu.SemaphoreType.DMA((4,)),
                pltpu.SemaphoreType.DMA((8,)),
                pltpu.SemaphoreType.DMA((8,)),
            ],
            compiler_params=pltpu.CompilerParams(
                collective_id=0, has_side_effects=True, vmem_limit_bytes=60 << 20
            ),
            name="ice",
        )(*arguments)

    return jax.shard_map(
        body,
        mesh=mesh,
        in_specs=placed,
        out_specs=(P(None, "mp", "server"), P("mp", "server", None, None, None)),
        check_vma=False,
    )
```

```python
import functools

import jax
import jax.numpy as jnp
from jax import lax
from jax.experimental import pallas as pl
from jax.experimental.pallas import tpu as pltpu
from jax.sharding import PartitionSpec as P

MESH = pl.DeviceIdType.MESH

CY, CX = 64, 128
ITERS = 20
HALO = 2 * ITERS
ROWS = CY + 2 * HALO
PAD = 8
FIELDS = 9
CAP, OFFSETS, BLOCKS, CROSS = 8, 5, 8, 4

RELAXATION = 0.1
STEP_SIZE = 0.3
DRAG_RATE = 1.0
FRAC_FLOOR = 0.3
KEEP_S = 1.0 / (1.0 + RELAXATION)
KEEP_V = 1.0 / (1.0 + STEP_SIZE * DRAG_RATE)
LOAD_SCALE = RELAXATION * 0.5 * KEEP_S
FORCE_SCALE = STEP_SIZE * KEEP_V * 0.25
WIND_SCALE = STEP_SIZE * KEEP_V
TINY = 1e-30

OWN_LANE = HALO // 2
RIGHT_LANE = (HALO + CX) // 2
SIDE_ROWS = 3 * CY
CORNER_ROWS = 80
EDGE_ROWS = 368
WIDTHS = (40, 32, 24, 16, 8)
STARTS = (0, 40, 72, 96, 112)
PLACE, BACK, SIDE, CORNER = 0, 256, 384, 1152

SPATIAL = ((0, -1), (0, 1), (-1, 0), (1, 0), (-1, -1), (-1, 1), (1, -1), (1, 1))
AROUND = SPATIAL + ((-2, 0), (2, 0)) + tuple((0, k) for k in range(2, 7))


def ones_where(condition):
    return jnp.where(condition, 1.0, 0.0).astype(jnp.bfloat16)


def fill_packing(packing):
    row = lax.broadcasted_iota(jnp.int32, (CX, CX), 0)
    shift = lax.broadcasted_iota(jnp.int32, (CX, CX), 1) - row
    slots = [(HALO, HALO * k) for k in range(3)] + list(zip(WIDTHS, STARTS))
    for i, (width, start) in enumerate(slots):
        rows = slice(i * CX, (i + 1) * CX)
        packing[rows, :CX] = ones_where((shift == start) & (row < width))
        packing[rows, CX:] = ones_where((shift == start - CX + width) & (row >= CX - width))


def fill_placing(placing):
    row = lax.broadcasted_iota(jnp.int32, (CX, CX), 0)
    column = lax.broadcasted_iota(jnp.int32, (CX, CX), 1)
    forth, back = 2 * column - row, 2 * row - column
    slots = [(SIDE + 2 * CX * k, HALO, HALO * k, 0) for k in range(3)]
    slots += [(CORNER + 2 * CX * g, WIDTHS[g], STARTS[g], 4 * g) for g in range(5)]
    for odd in range(2):
        own = ones_where(forth == HALO - odd)
        for half in range(2):
            placing[half * CX : (half + 1) * CX, PLACE + odd * CX : PLACE + (odd + 1) * CX] = own
        placing[odd * CX : (odd + 1) * CX, BACK:SIDE] = ones_where(back == HALO - odd)
        for at, width, start, lane in slots:
            columns = slice(at + odd * CX, at + (odd + 1) * CX)
            for half, first in enumerate((lane, RIGHT_LANE)):
                inside = (column >= first) & (column < first + width // 2)
                placing[half * CX : (half + 1) * CX, columns] = ones_where((forth == 2 * first - start - odd) & inside)


def split(x):
    high = x.astype(jnp.bfloat16)
    return high, (x - high.astype(jnp.float32)).astype(jnp.bfloat16)


def picked(x, matrix):
    return jnp.dot(x, matrix, preferred_element_type=jnp.float32)


def kernel(
    n_mp,
    n_server,
    vel_hbm,
    stress_hbm,
    wind_hbm,
    strength_hbm,
    mass_hbm,
    mask_hbm,
    send_list_hbm,
    block_index_hbm,
    span_slot_hbm,
    weights_hbm,
    state_ref,
    written_ref,
    vel,
    stress,
    wind,
    strength,
    mass,
    mask,
    send_list,
    block_index,
    span_slot,
    weights,
    packing,
    placing,
    cells,
    moist,
    chosen,
    pressure,
    side_out,
    edge_out,
    corner_out,
    side_in,
    edge_in,
    corner_in,
    field_rows,
    rows_out,
    rows_in,
    rows_all,
    blocks_done,
    spans_out,
    spans_in,
    in_sem,
    weight_sem,
    halo_send,
    halo_recv,
    rows_send,
    rows_recv,
    spans_send,
    spans_recv,
):
    me_y, me_x = lax.axis_index("mp"), lax.axis_index("server")

    def device(dy, dx):
        return (lax.rem(me_y + dy + n_mp, n_mp), lax.rem(me_x + dx + n_server, n_server))

    def inside(dy, dx):
        found = None
        for step, at, count in ((dy, me_y, n_mp), (dx, me_x, n_server)):
            if step:
                there = at >= -step if step < 0 else at < count - step
                found = there if found is None else found & there
        return found

    def where_inside(dy, dx, action):
        there = inside(dy, dx)
        action() if there is None else pl.when(there)(action)

    barrier = pltpu.get_barrier_semaphore()
    greeted = jnp.int32(0)
    for dy, dx in AROUND:
        where_inside(
            dy,
            0,
            lambda dy=dy, dx=dx: pl.semaphore_signal(
                barrier, inc=1, device_id=device(dy, dx), device_id_type=MESH
            ),
        )
        greeted = greeted + (1 if dy == 0 else inside(dy, 0).astype(jnp.int32))

    loads = [
        pltpu.make_async_copy(source, target, in_sem.at[i])
        for i, (source, target) in enumerate(
            (
                (vel_hbm, vel),
                (stress_hbm, stress),
                (wind_hbm, wind),
                (strength_hbm, strength),
                (mass_hbm, mass),
                (mask_hbm, mask),
                (send_list_hbm, send_list),
                (block_index_hbm, block_index),
                (span_slot_hbm, span_slot),
            )
        )
    ]
    for load in loads:
        load.start()
    weight_load = pltpu.make_async_copy(weights_hbm, weights, weight_sem)
    weight_load.start()
    fill_packing(packing)
    for load in loads[:6]:
        load.wait()

    ice = mask[...].astype(jnp.float32)
    per_mass = ice / mass[...]
    own = [
        vel[0],
        vel[1],
        stress[0] + stress[1],
        stress[0] - stress[1],
        stress[2] * 2.0,
        strength[...] * ice * LOAD_SCALE,
        per_mass * FORCE_SCALE,
        wind[0] * per_mass * WIND_SCALE,
        wind[1] * per_mass * WIND_SCALE,
    ]
    spare = jnp.zeros((8, CX), jnp.float32)
    edge_out[0] = jnp.concatenate([x[:HALO] for x in own] + [spare], axis=0).astype(jnp.bfloat16)
    edge_out[1] = jnp.concatenate([x[CY - HALO :] for x in own] + [spare], axis=0).astype(jnp.bfloat16)
    halo = [
        pltpu.make_async_remote_copy(
            src_ref=source,
            dst_ref=target,
            send_sem=halo_send.at[i],
            recv_sem=halo_recv.at[i],
            device_id=device(*SPATIAL[i]),
            device_id_type=MESH,
        )
        for i, (source, target) in enumerate(
            [(side_out.at[i], side_in.at[i]) for i in range(2)]
            + [(edge_out.at[i], edge_in.at[i]) for i in range(2)]
            + [(corner_out.at[i], corner_in.at[i]) for i in range(4)]
        )
    ]
    pl.semaphore_wait(barrier, greeted)

    def send_halo(i):
        where_inside(*SPATIAL[i], lambda: halo[i].start())

    def receive_halo(i):
        where_inside(*(-step for step in SPATIAL[i]), lambda: halo[i].wait_recv())


    highs = [split(x) for x in own]
    sides = jnp.concatenate(
        [jnp.concatenate([highs[3 * k + i][0] for k in range(3)], axis=1) for i in range(3)], axis=0
    )
    packets = picked(sides, packing[: 3 * CX]).astype(jnp.bfloat16)
    for i in range(2):
        side_out[i] = packets[:, i * CX : (i + 1) * CX]
        send_halo(i)
    ends = []
    for edge in range(2):
        groups = [
            jnp.concatenate([x[8 * g : 8 * g + 8] if edge == 0 else x[CY - 8 - 8 * g : CY - 8 * g] for x in own], axis=0)
            for g in range(5)
        ]
        ends.append(jnp.concatenate([jnp.concatenate([x, spare], axis=0) for x in groups], axis=1))
    corners = picked(jnp.concatenate(ends, axis=0).astype(jnp.bfloat16), packing[3 * CX :]).astype(jnp.bfloat16)
    for i in range(4):
        corner_out[i] = corners[CORNER_ROWS * (i // 2) : CORNER_ROWS * (i // 2 + 1), CX * (i % 2) : CX * (i % 2 + 1)]
        send_halo(4 + i)
    for i in (2, 3):
        send_halo(i)

    for f in range(FIELDS):
        for part in range(2):
            cells[f, part, 0:PAD] = spare
            cells[f, part, PAD + ROWS : PAD + ROWS + PAD] = spare
    fill_placing(placing)
    for f in range(FIELDS):
        placed = picked(jnp.concatenate(highs[f], axis=1), placing[:, PLACE:BACK])
        for part in range(2):
            cells[f, part, PAD + HALO : PAD + HALO + CY] = placed[:, part * CX : (part + 1) * CX]

    for load in loads[6:]:
        load.wait()
    column = lax.broadcasted_iota(jnp.int32, (8, 8 * CY), 1) - CY * lax.broadcasted_iota(jnp.int32, (8, 8 * CY), 0)
    for offset in range(OFFSETS):
        picks = [
            (column == send_list[0, offset, 0, slot]).astype(jnp.float32) for slot in range(CAP)
        ]
        chosen[offset * 64 : (offset + 1) * 64] = jnp.concatenate(picks, axis=0).astype(jnp.bfloat16)
    has_left, has_right = me_x > 0, me_x < n_server - 1
    has_up, has_down = me_y > 0, me_y < n_mp - 1

    def kept(ref, there):
        return jnp.where(there, ref[...].astype(jnp.float32), 0.0).astype(jnp.bfloat16)

    top, low = PAD, PAD + HALO + CY
    receive_halo(0)
    receive_halo(1)
    beside = jnp.concatenate([kept(side_in.at[1], has_left), kept(side_in.at[0], has_right)], axis=1)
    for k in range(3):
        found = picked(beside, placing[:, SIDE + 2 * CX * k : SIDE + 2 * CX * (k + 1)])
        for i in range(3):
            for part in range(2):
                cells[3 * k + i, part, PAD + HALO : low] += found[i * CY : (i + 1) * CY, part * CX : (part + 1) * CX]
    for which, start, there in ((1, top, has_up), (0, low, has_down)):
        receive_halo(2 + which)
        found = picked(kept(edge_in.at[which], there), placing[:CX, PLACE:BACK])
        for f in range(FIELDS):
            for part in range(2):
                cells[f, part, start : start + HALO] = found[f * HALO : (f + 1) * HALO, part * CX : (part + 1) * CX]
    for i in range(4, 8):
        receive_halo(i)
    for from_left, from_right, start, there in ((3, 2, top, has_up), (1, 0, low, has_down)):
        beyond = jnp.concatenate(
            [kept(corner_in.at[from_left], has_left & there), kept(corner_in.at[from_right], has_right & there)], axis=1
        )
        for g in range(5):
            found = picked(beyond, placing[:, CORNER + 2 * CX * g : CORNER + 2 * CX * (g + 1)])
            at = start + (HALO - 8 - 8 * g if start == top else 8 * g)
            for f in range(FIELDS):
                for part in range(2):
                    cells[f, part, at : at + 8] += found[f * 8 : (f + 1) * 8, part * CX : (part + 1) * CX]
    field_rows[6 * CY : 7 * CY] = mask[...].astype(jnp.bfloat16)
    field_rows[7 * CY : 8 * CY] = jnp.zeros((CY, CX), jnp.bfloat16)
    for part in range(2):
        moist[part] = jnp.where(cells[6, part] > 0.0, KEEP_V, 0.0)

    def across(even, odd):
        return odd - pltpu.roll(odd, 1, 1), pltpu.roll(even, CX - 1, 1) - even

    def stresses(start, count, keep_pressure):
        here, above, below = (pl.ds(start + d, count) for d in (0, -1, 1))
        u_x = across(*(cells[0, p, here] for p in range(2)))
        v_x = across(*(cells[1, p, here] for p in range(2)))
        for p in range(2):
            u_y = cells[0, p, below] - cells[0, p, above]
            v_y = cells[1, p, below] - cells[1, p, above]
            div, ten, shear = u_x[p] + v_y, u_x[p] - v_y, u_y + v_x[p]
            square = jnp.maximum(div * div + 0.25 * (ten * ten + shear * shear), TINY)
            deform = square * lax.rsqrt(square)
            bottom = deform + 1.0
            inverse = pl.reciprocal(bottom, approx=True)
            zeta = cells[5, p, here] * inverse
            one = zeta * (div - deform)
            two = (zeta * 0.25) * ten
            cells[2, p, here] = KEEP_S * cells[2, p, here] + (one + two)
            cells[3, p, here] = KEEP_S * cells[3, p, here] + (one - two)
            cells[4, p, here] = KEEP_S * cells[4, p, here] + (zeta * 0.5) * shear
            if keep_pressure:
                pressure[p, pl.ds(start - PAD - HALO, count)] = zeta * deform * (1.0 / LOAD_SCALE)

    def velocities(start, count):
        here, above, below = (pl.ds(start + d, count) for d in (0, -1, 1))
        p_x = across(*(cells[2, p, here] for p in range(2)))
        s_x = across(*(cells[4, p, here] for p in range(2)))
        for p in range(2):
            s_y = cells[4, p, below] - cells[4, p, above]
            m_y = cells[3, p, below] - cells[3, p, above]
            drag, keep = cells[6, p, here], moist[p, here]
            cells[0, p, here] = keep * cells[0, p, here] + ((p_x[p] + s_y) * drag + cells[7, p, here])
            cells[1, p, here] = keep * cells[1, p, here] + ((s_x[p] + m_y) * drag + cells[8, p, here])

    wave = []
    for step in range(ITERS):
        first, last, inner = step // 4, ROWS // 8 - step // 4, int(step % 4 == 3)
        wave += [(6 * step + group, 1, step, group) for group in range(first, last)]
        wave += [(6 * step + group + 3, 0, step, group) for group in range(first + inner, last - inner)]
    for _, is_stress, step, group in sorted(wave):
        if is_stress:
            stresses(PAD + 8 * group, 8, step == ITERS - 1 and HALO <= 8 * group < HALO + CY)
        else:
            velocities(PAD + 8 * group, 8)

    tile = slice(PAD + HALO, PAD + HALO + CY)

    def results(part):
        plus, minus = cells[2, part, tile], cells[3, part, tile]
        yield cells[0, part, tile]
        yield cells[1, part, tile]
        yield 0.5 * (plus + minus)
        yield 0.5 * (plus - minus)
        yield 0.5 * cells[4, part, tile]

    back = placing[:, BACK:SIDE]
    rests = []
    for f, pair in enumerate(zip(results(0), results(1))):
        high, rest = zip(*(split(x) for x in pair))
        rests.append(rest)
        rounded = picked(jnp.concatenate(high, axis=1), back)
        state_ref[f] = rounded
        field_rows[f * CY : (f + 1) * CY] = rounded.astype(jnp.bfloat16)
    ends = jnp.concatenate([pressure[p].astype(jnp.bfloat16) for p in range(2)], axis=1)
    field_rows[5 * CY : 6 * CY] = picked(ends, back).astype(jnp.bfloat16)

    rows_copies = []
    for order, offset in enumerate((0, 1, 3, 4, 2)):
        packet = jnp.dot(
            chosen[offset * 64 : (offset + 1) * 64], field_rows[...], preferred_element_type=jnp.float32
        )
        if offset == 2:
            rows_all[offset * CAP : (offset + 1) * CAP] = packet.reshape(CAP, 8, CX)
            continue
        rows_out[order] = packet.astype(jnp.bfloat16)
        copy = pltpu.make_async_remote_copy(
            src_ref=rows_out.at[order],
            dst_ref=rows_in.at[order],
            send_sem=rows_send.at[order],
            recv_sem=rows_recv.at[order],
            device_id=device(offset - 2, 0),
            device_id_type=MESH,
        )
        where_inside(offset - 2, 0, copy.start)
        rows_copies.append((order, offset, copy))
    for f, rest in enumerate(rests):
        state_ref[f] += picked(jnp.concatenate(rest, axis=1), back)
    weight_load.wait()
    for order, offset, copy in rows_copies:
        where_inside(2 - offset, 0, copy.wait_recv)
        rows_all[offset * CAP : (offset + 1) * CAP] = rows_in[order].astype(jnp.float32).reshape(CAP, 8, CX)

    for block in range(BLOCKS):
        source = jnp.concatenate(
            [rows_all[block_index[0, 0, cross, block]] for cross in range(CROSS)], axis=1
        ).astype(jnp.bfloat16)
        total = picked(source, weights[0, 0, block].reshape(CROSS * CX, CX))
        blocks_done[block] = total / jnp.maximum(total[6:7], FRAC_FLOOR)

    def for_span(span):
        found = jnp.zeros((8, CX), jnp.float32)
        for block in range(BLOCKS):
            found = jnp.where(span_slot[0, 0, block] == span, blocks_done[block], found)
        return found

    span_copies = []
    for hop in range(1, n_server):
        target = lax.rem(me_x + hop, n_server)
        spans_out[hop] = for_span(target)
        copy = pltpu.make_async_remote_copy(
            src_ref=spans_out.at[hop],
            dst_ref=spans_in.at[pl.ds(pl.multiple_of(me_x * 8, 8), 8)],
            send_sem=spans_send.at[hop],
            recv_sem=spans_recv.at[hop],
            device_id=(me_y, target),
            device_id_type=MESH,
        )
        copy.start()
        span_copies.append(copy)
    spans_in[pl.ds(pl.multiple_of(me_x * 8, 8), 8)] = for_span(me_x)
    for copy in span_copies:
        copy.wait_recv()
    for f in range(6):
        written_ref[0, 0, f] = spans_in[pl.ds(f, n_server, stride=8)]
    for i, copy in enumerate(halo):
        where_inside(*SPATIAL[i], copy.wait_send)
    for _, offset, copy in rows_copies:
        where_inside(offset - 2, 0, copy.wait_send)
    for copy in span_copies:
        copy.wait_send()


def solution(mesh):
    n_mp, n_server = mesh.shape["mp"], mesh.shape["server"]
    placed = (
        P(None, "mp", "server"),
        P(None, "mp", "server"),
        P(None, "mp", "server"),
        P("mp", "server"),
        P("mp", "server"),
        P("mp", "server"),
        P("mp", "server", None, None),
        P("mp", "server", None, None),
        P("mp", "server", None),
        P("mp", "server", None, None, None, None),
    )
    f32, bf16 = jnp.float32, jnp.bfloat16
    far = pl.BlockSpec(memory_space=pltpu.HBM)

    def body(*arguments):
        arguments = list(arguments)
        arguments[6] = jnp.transpose(arguments[6], (0, 2, 1, 3))
        arguments[7] = jnp.transpose(arguments[7], (0, 1, 3, 2))
        return pl.pallas_call(
            functools.partial(kernel, n_mp, n_server),
            out_shape=(
                pltpu.VMEM((5, CY, CX), f32),
                pltpu.VMEM((1, 1, 6, 8, CX), f32),
            ),
            in_specs=[far] * 10,
            out_specs=[pl.BlockSpec(memory_space=pltpu.VMEM)] * 2,
            scratch_shapes=[
                pltpu.VMEM((2, CY, CX), f32),
                pltpu.VMEM((3, CY, CX), f32),
                pltpu.VMEM((2, CY, CX), f32),
                pltpu.VMEM((CY, CX), f32),
                pltpu.VMEM((CY, CX), f32),
                pltpu.VMEM((CY, CX), jnp.int32),
                pltpu.SMEM((1, OFFSETS, 1, CAP), jnp.int32),
                pltpu.SMEM((1, 1, CROSS, BLOCKS), jnp.int32),
                pltpu.SMEM((1, 1, BLOCKS), jnp.int32),
                pltpu.VMEM((1, 1, BLOCKS, CROSS, CX, CX), bf16),
                pltpu.VMEM((8 * CX, 2 * CX), bf16),
                pltpu.VMEM((2 * CX, CORNER + 10 * CX), bf16),
                pltpu.VMEM((FIELDS, 2, ROWS + 2 * PAD, CX), f32),
                pltpu.VMEM((2, ROWS + 2 * PAD, CX), f32),
                pltpu.VMEM((OFFSETS * 64, 8 * CY), bf16),
                pltpu.VMEM((2, CY, CX), f32),
                pltpu.VMEM((2, SIDE_ROWS, CX), bf16),
                pltpu.VMEM((2, EDGE_ROWS, CX), bf16),
                pltpu.VMEM((4, CORNER_ROWS, CX), bf16),
                pltpu.VMEM((2, SIDE_ROWS, CX), bf16),
                pltpu.VMEM((2, EDGE_ROWS, CX), bf16),
                pltpu.VMEM((4, CORNER_ROWS, CX), bf16),
                pltpu.VMEM((8 * CY, CX), bf16),
                pltpu.VMEM((4, 64, CX), bf16),
                pltpu.VMEM((4, 64, CX), bf16),
                pltpu.VMEM((OFFSETS * CAP, 8, CX), f32),
                pltpu.VMEM((BLOCKS, 8, CX), f32),
                pltpu.VMEM((8, 8, CX), f32),
                pltpu.VMEM((64, CX), f32),
                pltpu.SemaphoreType.DMA((9,)),
                pltpu.SemaphoreType.DMA,
                pltpu.SemaphoreType.DMA((8,)),
                pltpu.SemaphoreType.DMA((8,)),
                pltpu.SemaphoreType.DMA((4,)),
                pltpu.SemaphoreType.DMA((4,)),
                pltpu.SemaphoreType.DMA((8,)),
                pltpu.SemaphoreType.DMA((8,)),
            ],
            compiler_params=pltpu.CompilerParams(
                collective_id=0, has_side_effects=True, vmem_limit_bytes=60 << 20
            ),
            name="ice",
        )(*arguments)

    return jax.shard_map(
        body,
        mesh=mesh,
        in_specs=placed,
        out_specs=(P(None, "mp", "server"), P("mp", "server", None, None, None)),
        check_vma=False,
    )
```
